1024 devices in a mesh: fsdp: 64 (over y, z_hi, core), head: 16 (over x, z_lo).
Axes of the slice: x: 8, y: 8, z: 8 (z_hi: 4, z_lo: 2; z = z_hi * 2 + z_lo), core: 2. Of those that a mesh axis runs over, the one named last changes fastest.
Arguments:
- query_up: bfloat16 [2, 1536, 128, 128], P(None, 'fsdp'), may hold values from -6 to 6
- key_up: bfloat16 [2, 512, 128, 128], P(None, 'head', 'fsdp'), may hold values from -0.5 to 0.5
Outputs:
- absorbed: bfloat16 [2, 128, 1536, 512], P(None, 'head', 'fsdp')
The draws below stay inside these ranges and needn't reach their ends.
All inputs are finite; a program needn't handle non-finite values.
Results may differ from the reference program's by a relative error of at most 0.001.
Values may be sent and summed in bfloat16 or wider, within the bound.
No kernel may reach another device: no remote copies, remote signals or barrier semaphores. Data moves between devices by JAX's collectives and lax.ppermute only.
A program may use at most 32 MiB of HBM per device.

```python
import jax
import jax.numpy as jnp
from jax import lax

H = 128
QR = 1536
LAT = 512
NOPE = 128
LAYERS = 2


def steps_of(key, extent, split, low, high):
    level = 1.0
    for dim, parts in split:
        draws = jax.random.uniform(jax.random.fold_in(jax.random.fold_in(key, 6), dim), (parts,), jnp.float32, low / len(split), high / len(split))
        level = level * jnp.repeat(jnp.exp(draws), extent[dim] // parts).reshape((-1,) + (1,) * (len(extent) - 1 - dim))
    return level


def noise(own_key, dims, deviation, limit, pieces=(), held_as=jnp.bfloat16):
    entries = deviation * jax.random.normal(own_key, dims, jnp.float32)
    if pieces:
        entries = entries * steps_of(own_key, dims, pieces, -0.22, 0.18)
    return jnp.clip(entries, -limit, limit).astype(held_as)


def setup_inputs(seed: int = 0) -> dict:
    arg_keys = jax.random.split(jax.random.key(seed), 3)
    query_up = noise(arg_keys[0], (LAYERS, QR, H, NOPE), 1.0, 6.0, ((1, 64),))
    key_up = noise(arg_keys[1], (LAYERS, LAT, H, NOPE), NOPE ** -0.5, 0.5, ((1, 16), (2, 64)))
    return {"query_up": query_up, "key_up": key_up}


def absorb_layer(weights):
    queries, keys = weights
    product = jnp.einsum("rhn,chn->hrc", queries.astype(jnp.float32), keys.astype(jnp.float32))
    return product.astype(jnp.bfloat16)


def reference(query_up, key_up):
    return lax.map(absorb_layer, (query_up, key_up))
```

```python
import itertools

import jax
import jax.numpy as jnp
from jax import lax
from jax.sharding import Mesh, PartitionSpec as P

AXES = ("yh", "yl", "zh", "core", "x", "zl")
SIZES = (4, 2, 4, 2, 8, 2)
QUERY = ("yh", "yl", "zh", "core")
HEAD = ("x", "zl")
PEERS = ("core", "yh", "yl")
BLOCKS = ("yl", "zh", "core")


def to_owner():
    index = {c: i for i, c in enumerate(itertools.product(*[range(s) for s in SIZES]))}
    pairs = []
    for (yh, yl, zh, core, x, zl), i in index.items():
        target = ((zh % 2) * 2 + core, x // 4, x % 4, zl, yh * 2 + yl, zh // 2)
        pairs.append((i, index[target]))
    return pairs


def shards(query_up, key_up):
    layers, rows, _, width = query_up.shape
    latent, pair = key_up.shape[1:3]

    held = lax.ppermute(key_up, AXES, to_owner())
    pieces = held.transpose(2, 0, 1, 3)
    pieces = jnp.broadcast_to(pieces[:, None], (pair, 4) + pieces.shape[1:])
    pieces = pieces.reshape(16, latent, width)
    keys = lax.all_to_all(pieces, BLOCKS, 0, 0, tiled=True).reshape(16 * latent, width)

    offset = lax.axis_index(HEAD) * 8
    own = lax.dynamic_slice_in_dim(query_up, offset, 8, 2)
    own = own.transpose(0, 2, 1, 3).reshape(16, rows, width)
    queries = lax.all_to_all(own, PEERS, 0, 0, tiled=True).reshape(16 * rows, width)

    product = lax.dot_general(queries, keys, (((1,), (1,)), ((), ())), preferred_element_type=jnp.float32)
    product = product.astype(jnp.bfloat16).reshape(16, rows, 16 * latent)
    out = lax.all_to_all(product, PEERS, 0, 0, tiled=True)
    return out.reshape(layers, 8, rows, 16 * latent)


def solution(mesh):
    fine = Mesh(mesh.devices.reshape(SIZES), AXES)
    return jax.shard_map(
        shards,
        mesh=fine,
        in_specs=(P(None, QUERY, None, None), P(None, HEAD, QUERY, None)),
        out_specs=P(None, HEAD, QUERY, None),
        check_vma=False,
    )
```

```python
import itertools

import jax
import jax.numpy as jnp
from jax import lax
from jax.experimental import pallas as pl
from jax.sharding import Mesh, PartitionSpec as P

AXES = ("yh", "yl", "zh", "core", "x", "zl")
SIZES = (4, 2, 4, 2, 8, 2)
QUERY = ("yh", "yl", "zh", "core")
HEAD = ("x", "zl")
PEERS = ("core", "yh", "yl")
BLOCKS = ("yl", "zh", "core")


def to_owner():
    index = {c: i for i, c in enumerate(itertools.product(*[range(s) for s in SIZES]))}
    pairs = []
    for (yh, yl, zh, core, x, zl), i in index.items():
        target = ((zh % 2) * 2 + core, x // 4, x % 4, zl, yh * 2 + yl, zh // 2)
        pairs.append((i, index[target]))
    return pairs


def copies(piece_ref, out_ref):
    for place in range(out_ref.shape[1]):
        out_ref[:, place] = piece_ref[...]


def spread(pieces, places):
    shape = (pieces.shape[0], places) + pieces.shape[1:]
    return pl.pallas_call(
        copies,
        out_shape=jax.ShapeDtypeStruct(shape, pieces.dtype),
        cost_estimate=pl.CostEstimate(flops=20_000_000_000, bytes_accessed=10 * pieces.size, transcendentals=0),
        name="spread",
    )(pieces)


def shards(query_up, key_up):
    layers, rows, _, width = query_up.shape
    latent, pair = key_up.shape[1:3]

    held = lax.ppermute(key_up, AXES, to_owner())
    pieces = held.transpose(2, 0, 1, 3)
    pieces = spread(pieces, 4).reshape(16, latent, width)
    keys = lax.all_to_all(pieces, BLOCKS, 0, 0, tiled=True).reshape(16 * latent, width)

    offset = lax.axis_index(HEAD) * 8
    own = lax.dynamic_slice_in_dim(query_up, offset, 8, 2)
    own = own.transpose(0, 2, 1, 3).reshape(16, rows, width)
    queries = lax.all_to_all(own, PEERS, 0, 0, tiled=True).reshape(16 * rows, width)

    product = lax.dot_general(queries, keys, (((1,), (1,)), ((), ())), preferred_element_type=jnp.float32)
    product = product.astype(jnp.bfloat16).reshape(16, rows, 16 * latent)
    out = lax.all_to_all(product, PEERS, 0, 0, tiled=True)
    return out.reshape(layers, 8, rows, 16 * latent)


def solution(mesh):
    fine = Mesh(mesh.devices.reshape(SIZES), AXES)
    return jax.shard_map(
        shards,
        mesh=fine,
        in_specs=(P(None, QUERY, None, None), P(None, HEAD, QUERY, None)),
        out_specs=P(None, HEAD, QUERY, None),
        check_vma=False,
    )
```

```python
import itertools

import jax
import jax.numpy as jnp
from jax import lax
from jax.experimental import pallas as pl
from jax.sharding import Mesh, PartitionSpec as P

AXES = ("y2", "y1", "y0", "zhh", "zhl", "core", "x", "zl")
SIZES = (2, 2, 2, 2, 2, 2, 8, 2)
QUERY = AXES[:6]
HEAD = ("x", "zl")
PAIR = ('y2', 'y1')
BLOCKS = ('core', 'y0', 'zhl', 'zhh')
ODD = 'y0'
LAYER = 'core'
PEERS = (LAYER,) + PAIR + (ODD,)


def to_owner():
    pairs = []
    index = {c: i for i, c in enumerate(itertools.product(*[range(s) for s in SIZES]))}
    for (y2, y1, y0, zhh, zhl, core, x, zl), i in index.items():
        place = dict(zip(PAIR, (zhl, core)))
        place.update(zip(BLOCKS, (x // 4, x // 2 % 2, x % 2, zl)))
        place.update(x=y2 * 4 + y1 * 2 + y0, zl=zhh)
        pairs.append((i, index[tuple(place[a] for a in AXES)]))
    return pairs


def copies(piece_ref, out_ref):
    for place in range(16):
        bits = dict(zip(BLOCKS, ((place >> s) % 2 for s in (3, 2, 1, 0))))
        if LAYER:
            out_ref[place] = piece_ref[bits[ODD] * 2 + bits[LAYER]]
        else:
            out_ref[place] = piece_ref[bits[ODD]]


def spread(pieces):
    shape = (16,) + pieces.shape[1:]
    return pl.pallas_call(
        copies,
        out_shape=jax.ShapeDtypeStruct(shape, pieces.dtype),
        cost_estimate=pl.CostEstimate(flops=20_000_000_000, bytes_accessed=10 * pieces.size, transcendentals=0),
        name="spread",
    )(pieces)


def shards(query_up, key_up):
    _, rows, _, width = query_up.shape
    latent = key_up.shape[1]

    held = lax.ppermute(key_up, AXES, to_owner())
    pieces = spread(held.transpose(2, 0, 1, 3).reshape(4, latent, width))
    keys = lax.all_to_all(pieces, BLOCKS, 0, 0, tiled=True)

    offset = lax.axis_index(HEAD) * 8
    own = lax.dynamic_slice_in_dim(query_up, offset, 8, 2)
    own = own.transpose(0, 2, 1, 3).reshape(16, rows, width)
    queries = lax.all_to_all(own, PEERS, 0, 0, tiled=True).reshape(16 * rows, width)
    keys = keys.reshape(16 * latent, width)
    product = lax.dot_general(queries, keys, (((1,), (1,)), ((), ())), preferred_element_type=jnp.float32)
    product = product.astype(jnp.bfloat16).reshape(16, rows, 16 * latent)
    out = lax.all_to_all(product, PEERS, 0, 0, tiled=True)
    return out.reshape(2, 8, rows, 16 * latent)


def solution(mesh):
    fine = Mesh(mesh.devices.reshape(SIZES), AXES)
    return jax.shard_map(
        shards,
        mesh=fine,
        in_specs=(P(None, QUERY, None, None), P(None, HEAD, QUERY, None)),
        out_specs=P(None, HEAD, QUERY, None),
        check_vma=False,
    )
```

```python
import itertools

import jax
import jax.numpy as jnp
from jax import lax
from jax.experimental import pallas as pl
from jax.experimental.pallas import tpu as pltpu
from jax.sharding import Mesh, PartitionSpec as P

AXES = ("y2", "y1", "y0", "zhh", "zhl", "core", "x", "zl")
SIZES = (2, 2, 2, 2, 2, 2, 8, 2)
QUERY = AXES[:6]
HEAD = ("x", "zl")
PAIR = ('y2', 'y1')
BLOCKS = ('core', 'y0', 'zhl', 'zhh')
ODD = 'y0'
LAYER = 'core'
PEERS = (LAYER,) + PAIR + (ODD,)


def to_owner():
    pairs = []
    index = {c: i for i, c in enumerate(itertools.product(*[range(s) for s in SIZES]))}
    for (y2, y1, y0, zhh, zhl, core, x, zl), i in index.items():
        place = dict(zip(PAIR, (zhl, core)))
        place.update(zip(BLOCKS, (x // 4, x // 2 % 2, x % 2, zl)))
        place.update(x=y2 * 4 + y1 * 2 + y0, zl=zhh)
        pairs.append((i, index[tuple(place[a] for a in AXES)]))
    return pairs


def copies(piece_ref, out_ref):
    for place in range(16):
        bits = dict(zip(BLOCKS, ((place >> s) % 2 for s in (3, 2, 1, 0))))
        if LAYER:
            out_ref[place] = piece_ref[bits[ODD] * 2 + bits[LAYER]]
        else:
            out_ref[place] = piece_ref[bits[ODD]]


def spread(pieces):
    shape = (16,) + pieces.shape[1:]
    return pl.pallas_call(
        copies,
        out_shape=jax.ShapeDtypeStruct(shape, pieces.dtype),
        compiler_params=pltpu.CompilerParams(vmem_limit_bytes=1 << 20),
        cost_estimate=pl.CostEstimate(flops=20_000_000_000, bytes_accessed=10 * pieces.size, transcendentals=0),
        name="spread",
    )(pieces)


def shards(query_up, key_up):
    _, rows, _, width = query_up.shape
    latent = key_up.shape[1]

    held = lax.ppermute(key_up, AXES, to_owner())
    pieces = spread(held.transpose(2, 0, 1, 3).reshape(4, latent, width))
    keys = lax.all_to_all(pieces, BLOCKS, 0, 0, tiled=True)

    offset = lax.axis_index(HEAD) * 8
    own = lax.dynamic_slice_in_dim(query_up, offset, 8, 2)
    own = own.transpose(0, 2, 1, 3).reshape(16, rows, width)
    queries = lax.all_to_all(own, PEERS, 0, 0, tiled=True).reshape(16 * rows, width)
    keys = keys.reshape(16 * latent, width)
    product = lax.dot_general(queries, keys, (((1,), (1,)), ((), ())), preferred_element_type=jnp.float32)
    product = product.astype(jnp.bfloat16).reshape(16, rows, 16 * latent)
    out = lax.all_to_all(product, PEERS, 0, 0, tiled=True)
    return out.reshape(2, 8, rows, 16 * latent)


def solution(mesh):
    fine = Mesh(mesh.devices.reshape(SIZES), AXES)
    return jax.shard_map(
        shards,
        mesh=fine,
        in_specs=(P(None, QUERY, None, None), P(None, HEAD, QUERY, None)),
        out_specs=P(None, HEAD, QUERY, None),
        check_vma=False,
    )
```

```python
import itertools

import jax
import jax.numpy as jnp
from jax import lax
from jax.experimental import pallas as pl
from jax.experimental.pallas import tpu as pltpu
from jax.sharding import Mesh, PartitionSpec as P

AXES = ("y2", "y1", "y0", "zhh", "zhl", "core", "x", "zl")
SIZES = (2, 2, 2, 2, 2, 2, 8, 2)
QUERY = AXES[:6]
HEAD = ("x", "zl")
PAIR = ('y2', 'y1')
BLOCKS = ('core', 'zhl', 'y0', 'zhh')
ODD = 'y0'
LAYER = 'core'
PEERS = (LAYER,) + PAIR + (ODD,)


def to_owner():
    pairs = []
    index = {c: i for i, c in enumerate(itertools.product(*[range(s) for s in SIZES]))}
    for (y2, y1, y0, zhh, zhl, core, x, zl), i in index.items():
        place = dict(zip(PAIR, (zhl, core)))
        place.update(zip(BLOCKS, (x // 4, x // 2 % 2, x % 2, zl)))
        place.update(x=y2 * 4 + y1 * 2 + y0, zl=zhh)
        pairs.append((i, index[tuple(place[a] for a in AXES)]))
    return pairs


def copies(piece_ref, out_ref):
    for place in range(16):
        bits = dict(zip(BLOCKS, ((place >> s) % 2 for s in (3, 2, 1, 0))))
        if LAYER:
            out_ref[place] = piece_ref[bits[ODD] * 2 + bits[LAYER]]
        else:
            out_ref[place] = piece_ref[bits[ODD]]


def spread(pieces):
    shape = (16,) + pieces.shape[1:]
    return pl.pallas_call(
        copies,
        out_shape=jax.ShapeDtypeStruct(shape, pieces.dtype),
        compiler_params=pltpu.CompilerParams(vmem_limit_bytes=1 << 20),
        cost_estimate=pl.CostEstimate(flops=20_000_000_000, bytes_accessed=10 * pieces.size, transcendentals=0),
        name="spread",
    )(pieces)


def shards(query_up, key_up):
    _, rows, _, width = query_up.shape
    latent = key_up.shape[1]

    held = lax.ppermute(key_up, AXES, to_owner())
    pieces = spread(held.transpose(2, 0, 1, 3).reshape(4, latent, width))
    keys = lax.all_to_all(pieces, BLOCKS, 0, 0, tiled=True)

    offset = lax.axis_index(HEAD) * 8
    own = lax.dynamic_slice_in_dim(query_up, offset, 8, 2)
    own = own.transpose(0, 2, 1, 3).reshape(16, rows, width)
    queries = lax.all_to_all(own, PEERS, 0, 0, tiled=True).reshape(16 * rows, width)
    keys = keys.reshape(16 * latent, width)
    product = lax.dot_general(queries, keys, (((1,), (1,)), ((), ())), preferred_element_type=jnp.float32)
    product = product.astype(jnp.bfloat16).reshape(16, rows, 16 * latent)
    out = lax.all_to_all(product, PEERS, 0, 0, tiled=True)
    return out.reshape(2, 8, rows, 16 * latent)


def solution(mesh):
    fine = Mesh(mesh.devices.reshape(SIZES), AXES)
    return jax.shard_map(
        shards,
        mesh=fine,
        in_specs=(P(None, QUERY, None, None), P(None, HEAD, QUERY, None)),
        out_specs=P(None, HEAD, QUERY, None),
        check_vma=False,
    )
```

```python
import itertools

import jax
import jax.numpy as jnp
from jax import lax
from jax.experimental import pallas as pl
from jax.experimental.pallas import tpu as pltpu
from jax.sharding import Mesh, PartitionSpec as P

AXES = ("y2", "y1", "y0", "zhh", "zhl", "core", "x", "zl")
SIZES = (2, 2, 2, 2, 2, 2, 8, 2)
QUERY = AXES[:6]
HEAD = ("x", "zl")
PAIR = ('y1', 'y2')
BLOCKS = ('core', 'zhl', 'y0', 'zhh')
ODD = 'y0'
LAYER = 'core'
PEERS = (LAYER,) + PAIR + (ODD,)


def to_owner():
    pairs = []
    index = {c: i for i, c in enumerate(itertools.product(*[range(s) for s in SIZES]))}
    for (y2, y1, y0, zhh, zhl, core, x, zl), i in index.items():
        place = dict(zip(PAIR, (zhl, core)))
        place.update(zip(BLOCKS, (x // 4, x // 2 % 2, x % 2, zl)))
        place.update(x=y2 * 4 + y1 * 2 + y0, zl=zhh)
        pairs.append((i, index[tuple(place[a] for a in AXES)]))
    return pairs


def copies(piece_ref, out_ref):
    for place in range(16):
        bits = dict(zip(BLOCKS, ((place >> s) % 2 for s in (3, 2, 1, 0))))
        if LAYER:
            out_ref[place] = piece_ref[bits[ODD] * 2 + bits[LAYER]]
        else:
            out_ref[place] = piece_ref[bits[ODD]]


def spread(pieces):
    shape = (16,) + pieces.shape[1:]
    return pl.pallas_call(
        copies,
        out_shape=jax.ShapeDtypeStruct(shape, pieces.dtype),
        compiler_params=pltpu.CompilerParams(vmem_limit_bytes=1 << 20),
        cost_estimate=pl.CostEstimate(flops=20_000_000_000, bytes_accessed=10 * pieces.size, transcendentals=0),
        name="spread",
    )(pieces)


def shards(query_up, key_up):
    _, rows, _, width = query_up.shape
    latent = key_up.shape[1]

    held = lax.ppermute(key_up, AXES, to_owner())
    pieces = spread(held.transpose(2, 0, 1, 3).reshape(4, latent, width))
    keys = lax.all_to_all(pieces, BLOCKS, 0, 0, tiled=True)

    offset = lax.axis_index(HEAD) * 8
    own = lax.dynamic_slice_in_dim(query_up, offset, 8, 2)
    own = own.transpose(0, 2, 1, 3).reshape(16, rows, width)
    queries = lax.all_to_all(own, PEERS, 0, 0, tiled=True).reshape(16 * rows, width)
    keys = keys.reshape(16 * latent, width)
    product = lax.dot_general(queries, keys, (((1,), (1,)), ((), ())), preferred_element_type=jnp.float32)
    product = product.astype(jnp.bfloat16).reshape(16, rows, 16 * latent)
    out = lax.all_to_all(product, PEERS, 0, 0, tiled=True)
    return out.reshape(2, 8, rows, 16 * latent)


def solution(mesh):
    fine = Mesh(mesh.devices.reshape(SIZES), AXES)
    return jax.shard_map(
        shards,
        mesh=fine,
        in_specs=(P(None, QUERY, None, None), P(None, HEAD, QUERY, None)),
        out_specs=P(None, HEAD, QUERY, None),
        check_vma=False,
    )
```

```python
import itertools

import jax
import jax.numpy as jnp
from jax import lax
from jax.experimental import pallas as pl
from jax.experimental.pallas import tpu as pltpu
from jax.sharding import Mesh, PartitionSpec as P

AXES = ("y2", "y1", "y0", "zhh", "zhl", "core", "x", "zl")
SIZES = (2, 2, 2, 2, 2, 2, 8, 2)
QUERY = AXES[:6]
HEAD = ("x", "zl")
PAIR = ('y1', 'y2')
BLOCKS = ('zhl', 'core', 'y0', 'zhh')
ODD = 'y0'
LAYER = 'core'
PEERS = (LAYER,) + PAIR + (ODD,)


def to_owner():
    pairs = []
    index = {c: i for i, c in enumerate(itertools.product(*[range(s) for s in SIZES]))}
    for (y2, y1, y0, zhh, zhl, core, x, zl), i in index.items():
        place = dict(zip(PAIR, (zhl, core)))
        place.update(zip(BLOCKS, (x // 4, x // 2 % 2, x % 2, zl)))
        place.update(x=y2 * 4 + y1 * 2 + y0, zl=zhh)
        pairs.append((i, index[tuple(place[a] for a in AXES)]))
    return pairs


def copies(piece_ref, out_ref):
    for place in range(16):
        bits = dict(zip(BLOCKS, ((place >> s) % 2 for s in (3, 2, 1, 0))))
        if LAYER:
            out_ref[place] = piece_ref[bits[ODD] * 2 + bits[LAYER]]
        else:
            out_ref[place] = piece_ref[bits[ODD]]


def spread(pieces):
    shape = (16,) + pieces.shape[1:]
    return pl.pallas_call(
        copies,
        out_shape=jax.ShapeDtypeStruct(shape, pieces.dtype),
        compiler_params=pltpu.CompilerParams(vmem_limit_bytes=1 << 20),
        cost_estimate=pl.CostEstimate(flops=20_000_000_000, bytes_accessed=10 * pieces.size, transcendentals=0),
        name="spread",
    )(pieces)


def shards(query_up, key_up):
    _, rows, _, width = query_up.shape
    latent = key_up.shape[1]

    held = lax.ppermute(key_up, AXES, to_owner())
    pieces = spread(held.transpose(2, 0, 1, 3).reshape(4, latent, width))
    keys = lax.all_to_all(pieces, BLOCKS, 0, 0, tiled=True)

    offset = lax.axis_index(HEAD) * 8
    own = lax.dynamic_slice_in_dim(query_up, offset, 8, 2)
    own = own.transpose(0, 2, 1, 3).reshape(16, rows, width)
    queries = lax.all_to_all(own, PEERS, 0, 0, tiled=True).reshape(16 * rows, width)
    keys = keys.reshape(16 * latent, width)
    product = lax.dot_general(queries, keys, (((1,), (1,)), ((), ())), preferred_element_type=jnp.float32)
    product = product.astype(jnp.bfloat16).reshape(16, rows, 16 * latent)
    out = lax.all_to_all(product, PEERS, 0, 0, tiled=True)
    return out.reshape(2, 8, rows, 16 * latent)


def solution(mesh):
    fine = Mesh(mesh.devices.reshape(SIZES), AXES)
    return jax.shard_map(
        shards,
        mesh=fine,
        in_specs=(P(None, QUERY, None, None), P(None, HEAD, QUERY, None)),
        out_specs=P(None, HEAD, QUERY, None),
        check_vma=False,
    )
```
